512 devices in a mesh: rep: 8 (over z), ep: 64 (over x, y, core).
Axes of the slice: x: 4, y: 8, z: 8, core: 2. Of those that a mesh axis runs over, the one named last changes fastest.
Arguments:
- queries: bfloat16 [2048, 2, 64, 576], P(('rep', 'ep')), may hold values from -8 to 8
- latent_key_cache: bfloat16 [2048, 256, 576], P(('rep', 'ep')), may hold values from -5 to 5
- fresh_latent_keys: bfloat16 [2048, 2, 576], P(('rep', 'ep')), may hold values from -5 to 5
- lengths: int32 [2048], P(('rep', 'ep')), may hold values from 64 to 256
- accepted: int32 [2048], P(('rep', 'ep')), may hold values 0 or 1
- hidden: bfloat16 [2048, 2, 3584], P(('rep', 'ep')), may hold values from -6 to 6
- norm_gain: float32 [3584], replicated, may hold values from 0.5 to 1.5
- expert_ids: int32 [2048, 2, 8], P(('rep', 'ep')), may hold values from 0 to 63, all different within a row; in each aligned block of 8 rows (0 to 7, 8 to 15, ..., all dimensions but the last counted through in order) at most 2 rows name the same one
- router_weights: bfloat16 [2048, 2, 8], P(('rep', 'ep')), may hold values from 0.099609375 to 0.59765625
- gate_weight: bfloat16 [64, 3584, 1024], P('ep', None, 'rep'), may hold values from -0.09375 to 0.09375
- up_weight: bfloat16 [64, 3584, 1024], P('ep', None, 'rep'), may hold values from -0.09375 to 0.09375
- down_weight: bfloat16 [64, 1024, 3584], P('ep', None, 'rep'), may hold values from -0.1875 to 0.1875
Outputs:
- attended: bfloat16 [2048, 2, 64, 512], P(('rep', 'ep'))
- routed: bfloat16 [2048, 2, 3584], P(('rep', 'ep'))
The draws below stay inside these ranges and needn't reach their ends.
Inputs may be any that keep to these rules, and one draw needn't show every extreme that they name: `expert_ids`: within the rows of one device (aligned blocks of 8 rows) no expert is named by more than 2 rows, and each row names different experts.
All inputs are finite; a program needn't handle non-finite values. No bound on the sum of `accepted` on one device may be relied on, other than what follows from the above.
Results may differ from the reference program's by a relative error of at most 0.0071.
Values may be sent and summed in bfloat16 or wider, within the bound.
No kernel may reach another device: no remote copies, remote signals or barrier semaphores. Data moves between devices by JAX's collectives and lax.ppermute only.
A program may use at most 64 MiB of HBM per device.

```python
import math
import jax
import jax.numpy as jnp
import numpy as np
from jax import lax

MODEL_WIDTH = 3584
FF = 1024
HEADS = 64
LATENT_WIDTH = 512
ROTARY_WIDTH = 64
TOPK = 8
ROWS_REQ = 2
REQ_DEV = 4
CACHE_SLOTS = 256
CAP = 2
KC = 576
REQUEST_TOTAL = 2048
ROUTED_EXPERTS = 64


def draw_latent_key_cache(key, part):
    key = jax.random.fold_in(key, 1)
    array_shape = (REQUEST_TOTAL, CACHE_SLOTS, LATENT_WIDTH + ROTARY_WIDTH)
    base = jnp.clip(jax.random.normal(key, array_shape, jnp.float32), -5.0, 5.0)
    return base.astype(jnp.bfloat16)


def draw_queries(key, part):
    key = jax.random.fold_in(key, 2)
    feature_width = LATENT_WIDTH + ROTARY_WIDTH
    array_shape = (REQUEST_TOTAL, ROWS_REQ, HEADS, feature_width)
    base = jnp.clip(jax.random.normal(key, array_shape, jnp.float32), -5.0, 5.0)
    return base.astype(jnp.bfloat16)


def draw_lengths(key, part):
    key = jax.random.fold_in(key, 3)
    first, second = jax.random.split(key)
    drawn = jax.random.randint(first, (REQUEST_TOTAL,), CACHE_SLOTS // 4, CACHE_SLOTS + 1)
    fullest = jax.random.randint(second, (), 0, REQUEST_TOTAL)
    return jnp.where(jnp.arange(REQUEST_TOTAL) == fullest, CACHE_SLOTS, drawn).astype(jnp.int32)


def with_ends(values, stream_key, smallest, high):
    shape = values.shape
    index_at = [jax.random.randint(jax.random.fold_in(stream_key, axis), (), 0, shape[axis]) for axis in range(len(shape))]
    values = values.at[tuple(index_at)].set(smallest)
    longest = shape.index(max(shape))
    index_at[longest] = (index_at[longest] + 1) % shape[longest]
    return values.at[tuple(index_at)].set(high)


def shard_levels(stream_key, dims, shards, smallest, largest):
    def one(dim, shards_of):
        draws = jax.random.uniform(jax.random.fold_in(jax.random.fold_in(stream_key, 6), dim), (shards_of,), jnp.float32, smallest / len(shards), largest / len(shards))
        return jnp.repeat(jnp.exp(draws), dims[dim] // shards_of).reshape((-1,) + (1,) * (len(dims) - dim - 1))

    loudness = one(*shards[0])
    for cut in shards[1:]:
        loudness = loudness * one(*cut)
    return loudness


def deal_out(stream_key, own, number, rows, number_of, top, limit, skew):
    sequence = jax.random.permutation(stream_key, number_of)
    heavy_load, usual = shares(number_of, rows * top, limit, skew, True), shares(number_of, rows * top, limit, skew, False)
    places = jnp.arange(number_of)

    def named(sizes, rotation):
        used = int((sizes > 0).sum())
        fixed = max(1, used // 4)
        moved = fixed + (places - fixed + rotation * (used - fixed)) % max(1, number_of - fixed)
        return jnp.zeros((number_of,), jnp.int32).at[sequence[jnp.where(places < fixed, places, moved)]].set(jnp.asarray(sizes, jnp.int32))

    sizes = jnp.where(number % 4 == 0, named(heavy_load, number // 4), named(usual, number - number // 4 - 1))
    mixed = jax.random.permutation(jax.random.fold_in(own, 3), number_of)
    giver, receiver = mixed[0:number_of // 2 * 2:2], mixed[1:number_of // 2 * 2:2]
    room = jnp.minimum(sizes[giver] - 1, limit - sizes[receiver]) // 2
    room = jnp.where((giver == sequence[0]) | (receiver == sequence[0]) | (sizes[receiver] == 0), 0, jnp.maximum(room, 0))
    moved = jax.random.randint(jax.random.fold_in(own, 4), (number_of // 2,), 0, 1 << 20) % (room + 1)
    sizes = sizes.at[giver].add(-moved).at[receiver].add(moved)
    labels = jnp.searchsorted(jnp.cumsum(sizes), jnp.arange(rows * top), side="right").astype(jnp.int32)
    table = labels.reshape(top, rows).T
    table = table[jax.random.permutation(jax.random.fold_in(own, 1), rows)]
    rotation = jax.random.randint(jax.random.fold_in(own, 2), (rows, 1), 0, top)
    return jnp.take_along_axis(table, (jnp.arange(top)[None, :] + rotation) % top, axis=1)


def shares(number_of, total, reach, slope, full):
    weights = [(1 << 20) // math.isqrt(rank ** slope) + 1 for rank in range(1, number_of + 1)]
    largest = reach if full else min(reach, max(-(-total // number_of), total * weights[0] // sum(weights)))
    least = 1 if total - largest >= number_of - 1 else 0
    given, rest = [largest] + [least] * (number_of - 1), total - largest - least * (number_of - 1)
    while rest > 0:
        movable = [i for i in range(1, number_of) if given[i] < largest] or [i for i in range(1, number_of) if given[i] < reach]
        mass, left = sum([weights[i] for i in movable]), rest
        for i in movable:
            more = min(reach - given[i], max(1, left * weights[i] // mass), rest)
            given[i] = given[i] + more
            rest = rest - more
    return np.array(given)


def scatter_about(key, extent, width, reach, pieces=(), kind=jnp.bfloat16):
    level = shard_levels(key, extent, pieces, -0.22, 0.18) if pieces else 1.0
    values = jax.random.normal(key, extent, jnp.float32) * width * level
    return jnp.minimum(jnp.maximum(values, -reach), reach).astype(kind)


def setup_inputs(seed: int = 0) -> dict:
    streams_of = jax.random.split(jax.random.key(seed), 13)
    queries = draw_queries(jax.random.fold_in(streams_of[12], 71), 0)
    latent_key_cache = draw_latent_key_cache(jax.random.fold_in(streams_of[12], 71), 0)
    fresh_latent_keys = scatter_about(streams_of[2], (REQUEST_TOTAL, ROWS_REQ, KC), 1.0, 5.0, ((0, 512),))
    lengths = draw_lengths(jax.random.fold_in(streams_of[12], 71), 0)
    accepted = with_ends((jax.random.randint(streams_of[4], (REQUEST_TOTAL,), 0, 4) < 3).astype(jnp.int32), jax.random.fold_in(streams_of[4], 1), 0, 1)
    hidden = scatter_about(streams_of[5], (REQUEST_TOTAL, ROWS_REQ, MODEL_WIDTH), 1.0, 6.0, ((0, 512),))
    norm_gain = jnp.clip(1.0 + 0.1 * jax.random.normal(streams_of[6], (MODEL_WIDTH,), jnp.float32), 0.5, 1.5)
    expert_ids_keys = jax.random.split(jax.random.fold_in(streams_of[7], 1), REQUEST_TOTAL * ROWS_REQ // (ROWS_REQ * REQ_DEV))
    expert_ids_turns = jax.random.permutation(jax.random.fold_in(streams_of[7], 3), REQUEST_TOTAL * ROWS_REQ // (ROWS_REQ * REQ_DEV))
    expert_ids = jax.vmap(lambda own, number: deal_out(jax.random.fold_in(streams_of[7], 2), own, number, ROWS_REQ * REQ_DEV, ROUTED_EXPERTS, TOPK, CAP, 2))(expert_ids_keys, expert_ids_turns).reshape((REQUEST_TOTAL, ROWS_REQ, TOPK))
    router_weights = jnp.clip(0.099609375 + 0.49804688 * jax.random.uniform(streams_of[8], (REQUEST_TOTAL, ROWS_REQ, TOPK), jnp.float32) ** shard_levels(streams_of[8], (REQUEST_TOTAL, ROWS_REQ, TOPK), ((0, 512),), -0.2, 0.2), 0.099609375, 0.59765625).astype(jnp.bfloat16)
    gate_weight = scatter_about(streams_of[9], (ROUTED_EXPERTS, MODEL_WIDTH, FF), MODEL_WIDTH ** -0.5, 0.09375, ((0, 64), (2, 8)))
    up_weight = scatter_about(streams_of[10], (ROUTED_EXPERTS, MODEL_WIDTH, FF), MODEL_WIDTH ** -0.5, 0.09375, ((0, 64), (2, 8)))
    down_weight = scatter_about(streams_of[11], (ROUTED_EXPERTS, FF, MODEL_WIDTH), FF ** -0.5, 0.1875, ((0, 64), (2, 8)))
    return {"queries": queries, "latent_key_cache": latent_key_cache, "fresh_latent_keys": fresh_latent_keys, "lengths": lengths, "accepted": accepted, "hidden": hidden, "norm_gain": norm_gain, "expert_ids": expert_ids, "router_weights": router_weights, "gate_weight": gate_weight, "up_weight": up_weight, "down_weight": down_weight}


score_scale = 192.0 ** (-0.5)
rows_per_block = 128

def attend_one(args):
    query, cache, own, length, live = args
    random_keys = jnp.concatenate([cache, own], 0)
    count = random_keys.shape[0]
    score = jnp.einsum('thc,kc->thk', query.astype(jnp.float32), random_keys.astype(jnp.float32)) * score_scale
    position = jnp.arange(count, dtype=jnp.int32)
    row = jnp.arange(2, dtype=jnp.int32)
    valid = (position[None, :] < length) | (position[None, :] == count - 2) | (position[None, :] == count - 1) & (row[:, None] == 1)
    score = jnp.where(valid[:, None, :], score, -jnp.inf)
    top = lax.optimization_barrier(jnp.max(score, -1, keepdims=True))
    expo = jnp.exp(score - top)
    prob = (expo / lax.optimization_barrier(jnp.sum(expo, -1, keepdims=True))).astype(jnp.bfloat16)
    value_rows = random_keys[:, :LATENT_WIDTH]
    out = jnp.einsum('thk,kc->thc', prob.astype(jnp.float32), value_rows.astype(jnp.float32))
    keep = jnp.stack([jnp.float32(1.0), live.astype(jnp.float32)])
    return (out * keep[:, None, None]).astype(jnp.bfloat16)

def reference(queries, latent_key_cache, fresh_latent_keys, lengths, accepted, hidden, norm_gain, expert_ids, router_weights, gate_weight, up_weight, down_weight):
    attended = lax.map(attend_one, (queries, latent_key_cache, fresh_latent_keys, lengths, accepted))
    rows = REQUEST_TOTAL * ROWS_REQ
    token_pairs = rows * TOPK
    x = hidden.reshape(rows, MODEL_WIDTH).astype(jnp.float32)
    meansq = lax.optimization_barrier(jnp.mean(x * x, -1, keepdims=True))
    normed = (x * lax.rsqrt(meansq + 1e-06) * norm_gain).astype(jnp.bfloat16)
    normed_pad = jnp.concatenate([normed, jnp.zeros((1, MODEL_WIDTH), jnp.bfloat16)], 0)
    row_live = jnp.stack([jnp.ones_like(accepted), accepted], 1).reshape(rows)
    pair_live = jnp.repeat(row_live, TOPK)
    ids = expert_ids.reshape(token_pairs)
    group = jnp.where(pair_live > 0, ids, ROUTED_EXPERTS).astype(jnp.int32)
    sorting_order = jnp.argsort(group, stable=True).astype(jnp.int32)
    counts = lax.optimization_barrier(jnp.sum((group[:, None] == jnp.arange(ROUTED_EXPERTS, dtype=jnp.int32)[None, :]).astype(jnp.int32), 0))
    padded = (counts + rows_per_block - 1) // rows_per_block * rows_per_block
    ends = jnp.cumsum(padded).astype(jnp.int32)
    group_starts = ends - padded
    first = (jnp.cumsum(counts) - counts).astype(jnp.int32)
    block_count = token_pairs // rows_per_block + ROUTED_EXPERTS
    slot_count = block_count * rows_per_block
    ordered_group = group[sorting_order]
    clamped_group = jnp.minimum(ordered_group, ROUTED_EXPERTS - 1)
    sorted_rank = jnp.arange(token_pairs, dtype=jnp.int32) - first[clamped_group]
    padding_position = jnp.where(ordered_group < ROUTED_EXPERTS, group_starts[clamped_group] + sorted_rank, slot_count).astype(jnp.int32)
    slot_to_pair = jnp.full((slot_count,), token_pairs, jnp.int32).at[padding_position].set(sorting_order, mode='drop')
    pairing_slot = jnp.full((token_pairs,), slot_count, jnp.int32).at[sorting_order].set(padding_position)
    pair_row = jnp.arange(token_pairs, dtype=jnp.int32) // TOPK
    slot_row = jnp.where(slot_to_pair < token_pairs, pair_row[jnp.minimum(slot_to_pair, token_pairs - 1)], rows).astype(jnp.int32)
    block_start = jnp.arange(block_count, dtype=jnp.int32) * rows_per_block
    block_expert = jnp.minimum(lax.optimization_barrier(jnp.sum((ends[None, :] <= block_start[:, None]).astype(jnp.int32), 1)), ROUTED_EXPERTS - 1).astype(jnp.int32)

    def process_block(index):
        take = lax.dynamic_slice_in_dim(slot_row, index * rows_per_block, rows_per_block)
        block = normed_pad[take]
        expert = block_expert[index]
        gate = jnp.dot(block, gate_weight[expert], preferred_element_type=jnp.float32)
        up = jnp.dot(block, up_weight[expert], preferred_element_type=jnp.float32)
        inner = (jax.nn.silu(gate) * up).astype(jnp.bfloat16)
        return jnp.dot(inner, down_weight[expert], preferred_element_type=jnp.float32).astype(jnp.bfloat16)
    output_rows = lax.map(process_block, jnp.arange(block_count, dtype=jnp.int32)).reshape(slot_count, MODEL_WIDTH)
    selected_experts = output_rows[jnp.minimum(pairing_slot, slot_count - 1)].astype(jnp.float32)
    weight = jnp.where(pair_live > 0, router_weights.reshape(token_pairs).astype(jnp.float32), 0.0)
    routed = lax.optimization_barrier(jnp.sum((selected_experts * weight[:, None]).reshape(rows, TOPK, MODEL_WIDTH), 1))
    return (attended, routed.reshape(REQUEST_TOTAL, ROWS_REQ, MODEL_WIDTH).astype(jnp.bfloat16))
```

```python
from functools import partial

import jax
import jax.numpy as jnp
from jax import lax
from jax.experimental import pallas as pl
from jax.experimental.pallas import tpu as pltpu
from jax.sharding import PartitionSpec as P

LATENT_WIDTH = 512

score_scale = 192.0 ** (-0.5)
SMEM = pl.BlockSpec(memory_space=pltpu.SMEM)
VMEM = pl.BlockSpec(memory_space=pltpu.VMEM)
limit = pltpu.CompilerParams(vmem_limit_bytes=48 * 1024 * 1024)


def prepare_kernel(hidden_ref, gain_ref, ids_ref, weights_ref, live_ref, rows_ref, mix_ref):
    rows, width = hidden_ref.shape
    x = hidden_ref[...].astype(jnp.float32)
    meansq = jnp.mean(x * x, -1, keepdims=True)
    normed = x * lax.rsqrt(meansq + 1e-06) * gain_ref[...]
    rows_ref[:, :width] = normed.astype(jnp.bfloat16)

    slots = mix_ref.shape[1]
    lane = lax.broadcasted_iota(jnp.int32, (rows, slots), 1)
    live = live_ref[...].astype(jnp.float32)
    named = jnp.zeros((rows, slots), jnp.float32)
    weight = jnp.zeros((rows, slots), jnp.float32)
    for p in range(ids_ref.shape[1]):
        hit = lane // 2 == ids_ref[:, p : p + 1]
        named += jnp.where(hit, live, 0.0)
        weight += jnp.where(hit, weights_ref[:, p : p + 1].astype(jnp.float32), 0.0)
    row = lax.broadcasted_iota(jnp.int32, (rows, slots), 0)
    rank = jnp.zeros((rows, slots), jnp.float32)
    for r in range(rows - 1):
        rank += jnp.where(row > r, named[r : r + 1, :], 0.0)
    taken = jnp.where(rank == (lane % 2).astype(jnp.float32), named, 0.0)
    rows_ref[:, width:] = taken.astype(jnp.bfloat16)
    mix_ref[...] = (taken * weight).astype(jnp.bfloat16)


def dispatch_kernel(rows_ref, out_ref):
    slots, width = out_ref.shape
    taken = rows_ref[:, width:]
    step = 512
    for c in range(0, width, step):
        out_ref[:, c : c + step] = lax.dot_general(
            taken,
            rows_ref[:, c : c + step],
            (((0,), (0,)), ((), ())),
            preferred_element_type=jnp.float32,
        ).astype(jnp.bfloat16)


def inner_piece(rows, weight):
    units = weight.shape[1] // 2
    both = jnp.dot(rows, weight, preferred_element_type=jnp.float32)
    g, u = both[:, :units], both[:, units:]
    return (g / (1.0 + jnp.exp(-g)) * u).astype(jnp.bfloat16)


def inner_kernel(weight_ref, *refs):
    out_ref = refs[-1]
    for i, rows_ref in enumerate(refs[:-1]):
        out_ref[i] = inner_piece(rows_ref[...], weight_ref[...])


def last_inner_kernel(places, me_ref, weight_ref, *refs):
    out_ref = refs[-1]
    count = out_ref.shape[0]
    new, old = refs[:2], refs[2:-1]
    for place, rows_ref in zip(places[:2], new):
        out_ref[lax.rem(me_ref[0] + place + count, count)] = inner_piece(
            rows_ref[...], weight_ref[...]
        )
    for i, place in enumerate(places[2:]):
        out_ref[lax.rem(me_ref[0] + place + count, count)] = old[i // 2][i % 2]


def down_kernel(inner_ref, weight_ref, out_ref):
    full = jnp.concatenate([inner_ref[r] for r in range(inner_ref.shape[0])], axis=1)
    out_ref[...] = lax.dot_general(
        full, weight_ref[...], (((1,), (1,)), ((), ())), preferred_element_type=jnp.float32
    ).astype(jnp.bfloat16)


def mix_kernel(mix_ref, back_ref, out_ref):
    out_ref[...] = jnp.dot(
        mix_ref[...], back_ref[...], preferred_element_type=jnp.float32
    ).astype(jnp.bfloat16)


def attend(queries, latent_key_cache, fresh_latent_keys, lengths, row_live):
    cache_len = latent_key_cache.shape[1]
    s_old = (
        jnp.einsum("rthc,rkc->rthk", queries, latent_key_cache, preferred_element_type=jnp.float32)
        * score_scale
    )
    s_new = (
        jnp.einsum("rthc,rnc->rthn", queries, fresh_latent_keys, preferred_element_type=jnp.float32)
        * score_scale
    )
    valid_old = jnp.arange(cache_len, dtype=jnp.int32)[None, :] < lengths[:, None]
    valid_new = jnp.arange(2, dtype=jnp.int32)[None, :] <= jnp.arange(2, dtype=jnp.int32)[:, None]
    s_old = jnp.where(valid_old[:, None, None, :], s_old, -jnp.inf)
    s_new = jnp.where(valid_new[None, :, None, :], s_new, -jnp.inf)
    top = jnp.maximum(jnp.max(s_old, -1, keepdims=True), jnp.max(s_new, -1, keepdims=True))
    e_old = jnp.exp(s_old - top)
    e_new = jnp.exp(s_new - top)
    total = jnp.sum(e_old, -1, keepdims=True) + jnp.sum(e_new, -1, keepdims=True)
    cached_probability = (e_old / total).astype(jnp.bfloat16)
    fresh_probability = (e_new / total).astype(jnp.bfloat16)
    out = jnp.einsum(
        "zlim,zmd->zlid",
        cached_probability,
        latent_key_cache[:, :, :LATENT_WIDTH],
        preferred_element_type=jnp.float32,
    )
    out = out + jnp.einsum(
        "swbd,sdo->swbo",
        fresh_probability,
        fresh_latent_keys[:, :, :LATENT_WIDTH],
        preferred_element_type=jnp.float32,
    )
    return (out * row_live.astype(jnp.float32)[:, :, None, None]).astype(jnp.bfloat16)


def per_device(
    queries,
    latent_key_cache,
    fresh_latent_keys,
    lengths,
    accepted,
    hidden,
    norm_gain,
    expert_ids,
    router_weights,
    gate_weight,
    up_weight,
    down_weight,
):
    nreq = queries.shape[0]
    width = hidden.shape[2]
    picks = expert_ids.shape[2]
    nrep = lax.axis_size("rep")
    experts = lax.axis_size("ep")
    rows = nreq * 2
    units = gate_weight.shape[2]
    slots = 2 * experts
    row_live = jnp.stack([jnp.ones_like(accepted), accepted], 1)
    attended = attend(queries, latent_key_cache, fresh_latent_keys, lengths, row_live)

    all_down = lax.all_gather(
        jnp.swapaxes(down_weight[0], 0, 1), "rep", axis=0, tiled=True
    )
    tagged, mix = pl.pallas_call(
        prepare_kernel,
        out_shape=(
            jax.ShapeDtypeStruct((rows, width + slots), jnp.bfloat16),
            jax.ShapeDtypeStruct((rows, slots), jnp.bfloat16),
        ),
        in_specs=[VMEM] * 5,
        out_specs=(VMEM, VMEM),
        compiler_params=limit,
        name="prepare",
    )(
        hidden.reshape(rows, width),
        norm_gain.reshape(1, width),
        expert_ids.reshape(rows, picks),
        router_weights.reshape(rows, picks),
        row_live.reshape(rows, 1),
    )

    def to_experts(rows_in):
        buffer = pl.pallas_call(
            dispatch_kernel,
            out_shape=jax.ShapeDtypeStruct((slots, width), jnp.bfloat16),
            in_specs=[VMEM],
            out_specs=VMEM,
            compiler_params=limit,
            name="dispatch",
        )(rows_in)
        moved = lax.all_to_all(
            buffer.reshape(experts, 2, width), "ep", split_axis=0, concat_axis=0, tiled=True
        )
        return moved.reshape(slots, width)

    def shift(x, by):
        return lax.ppermute(x, "rep", [(i, (i + by) % nrep) for i in range(nrep)])

    both_weight = jnp.concatenate([gate_weight[0], up_weight[0]], axis=1)

    def inner_blocks(*blocks):
        n = len(blocks)
        return pl.pallas_call(
            inner_kernel,
            out_shape=jax.ShapeDtypeStruct((n, slots, units), jnp.bfloat16),
            in_specs=[VMEM] * (n + 1),
            out_specs=VMEM,
            compiler_params=limit,
            cost_estimate=pl.CostEstimate(
                flops=4 * n * slots * width * units,
                bytes_accessed=2 * width * (2 * units + n * slots),
                transcendentals=n * slots * units,
            ),
            name="inner",
        )(both_weight, *blocks)

    own = to_experts(tagged)
    far = to_experts(shift(tagged, nrep // 2))
    places, done = [], []
    up_block = down_block = own
    for s in range(1, nrep // 2):
        up_block, down_block = shift(up_block, 1), shift(down_block, -1)
        places = places + [-s, s]
        if s < nrep // 2 - 1:
            done.append(inner_blocks(up_block, down_block))
    places = places[-2:] + places[:-2] + [0, nrep // 2]
    done.append(inner_blocks(own, far))
    by_home = pl.pallas_call(
        partial(last_inner_kernel, places),
        out_shape=jax.ShapeDtypeStruct((nrep, slots, units), jnp.bfloat16),
        in_specs=[SMEM] + [VMEM] * (3 + len(done)),
        out_specs=VMEM,
        compiler_params=limit,
        name="last_inner",
    )(
        lax.axis_index("rep").astype(jnp.int32).reshape(1),
        both_weight,
        up_block,
        down_block,
        *done,
    )
    inner = lax.all_to_all(by_home, "rep", split_axis=0, concat_axis=0, tiled=True)
    columns = 512
    expert_out = pl.pallas_call(
        down_kernel,
        out_shape=jax.ShapeDtypeStruct((slots, width), jnp.bfloat16),
        grid=(width // columns,),
        in_specs=[
            pl.BlockSpec((nrep, slots, units), lambda i: (0, 0, 0)),
            pl.BlockSpec((columns, nrep * units), lambda i: (i, 0)),
        ],
        out_specs=pl.BlockSpec((slots, columns), lambda i: (0, i)),
        compiler_params=limit,
        name="down",
    )(inner, all_down)
    back = lax.all_to_all(
        expert_out.reshape(experts, 2, width), "ep", split_axis=0, concat_axis=0, tiled=True
    ).reshape(slots, width)
    routed = pl.pallas_call(
        mix_kernel,
        out_shape=jax.ShapeDtypeStruct((rows, width), jnp.bfloat16),
        in_specs=[VMEM] * 2,
        out_specs=VMEM,
        compiler_params=limit,
        name="mix",
    )(mix, back)
    return attended, routed.reshape(nreq, 2, width)


def solution(mesh):
    in_specs = (
        P(("rep", "ep"), None, None, None),
        P(("rep", "ep"), None, None),
        P(("rep", "ep"), None, None),
        P(("rep", "ep")),
        P(("rep", "ep")),
        P(("rep", "ep"), None, None),
        P(),
        P(("rep", "ep"), None, None),
        P(("rep", "ep"), None, None),
        P("ep", None, "rep"),
        P("ep", None, "rep"),
        P("ep", None, "rep"),
    )
    out_specs = (P(("rep", "ep"), None, None, None), P(("rep", "ep"), None, None))
    return jax.shard_map(
        per_device, mesh=mesh, in_specs=in_specs, out_specs=out_specs, check_vma=False
    )
```

```python
from functools import partial

import jax
import jax.numpy as jnp
from jax import lax
from jax.experimental import pallas as pl
from jax.experimental.pallas import tpu as pltpu
from jax.sharding import PartitionSpec as P

LATENT_WIDTH = 512

score_scale = 192.0 ** (-0.5)
VMEM = pl.BlockSpec(memory_space=pltpu.VMEM)
limit = pltpu.CompilerParams(vmem_limit_bytes=48 * 1024 * 1024)


def prepare_kernel(hidden_ref, gain_ref, ids_ref, weights_ref, live_ref, rows_ref, mix_ref):
    rows, width = hidden_ref.shape
    x = hidden_ref[...].astype(jnp.float32)
    meansq = jnp.mean(x * x, -1, keepdims=True)
    normed = x * lax.rsqrt(meansq + 1e-06) * gain_ref[...]
    rows_ref[:, :width] = normed.astype(jnp.bfloat16)

    slots = mix_ref.shape[1]
    lane = lax.broadcasted_iota(jnp.int32, (rows, slots), 1)
    live = live_ref[...].astype(jnp.float32)
    named = jnp.zeros((rows, slots), jnp.float32)
    weight = jnp.zeros((rows, slots), jnp.float32)
    for p in range(ids_ref.shape[1]):
        hit = lane // 2 == ids_ref[:, p : p + 1]
        named += jnp.where(hit, live, 0.0)
        weight += jnp.where(hit, weights_ref[:, p : p + 1].astype(jnp.float32), 0.0)
    row = lax.broadcasted_iota(jnp.int32, (rows, slots), 0)
    rank = jnp.zeros((rows, slots), jnp.float32)
    for r in range(rows - 1):
        rank += jnp.where(row > r, named[r : r + 1, :], 0.0)
    taken = jnp.where(rank == (lane % 2).astype(jnp.float32), named, 0.0)
    rows_ref[:, width:] = taken.astype(jnp.bfloat16)
    mix_ref[...] = (taken * weight).astype(jnp.bfloat16)


def dispatch_kernel(rows_ref, out_ref):
    slots, width = out_ref.shape
    taken = rows_ref[:, width:]
    step = 512
    for c in range(0, width, step):
        out_ref[:, c : c + step] = lax.dot_general(
            taken,
            rows_ref[:, c : c + step],
            (((0,), (0,)), ((), ())),
            preferred_element_type=jnp.float32,
        ).astype(jnp.bfloat16)


def inner_piece(rows, weight):
    units = weight.shape[1] // 2
    both = jnp.dot(rows, weight, preferred_element_type=jnp.float32)
    g, u = both[:, :units], both[:, units:]
    return (g / (1.0 + jnp.exp(-g)) * u).astype(jnp.bfloat16)


def inner_kernel(have, weight_ref, *refs):
    out_ref = refs[-1]
    at = 0
    for ref in refs[:have]:
        for i in range(ref.shape[0]):
            out_ref[at] = ref[i]
            at += 1
    for rows_ref in refs[have:-1]:
        out_ref[at] = inner_piece(rows_ref[...], weight_ref[...])
        at += 1


def last_inner_kernel(weight_ref, *refs):
    out_ref = refs[-1]
    for i, rows_ref in enumerate(refs[:-1]):
        piece = inner_piece(rows_ref[...], weight_ref[...])
        for r in range(out_ref.shape[0]):
            out_ref[r, i] = piece


def down_kernel(first_places, last_places, first_ref, last_ref, weight_ref, out_ref):
    count, slots = first_ref.shape[0], first_ref.shape[2]

    def piece(r, home):
        place = (home - r) % count
        if place in first_places:
            return first_ref[r, first_places.index(place)]
        return last_ref[r, last_places.index(place)]

    for home in range(count):
        full = jnp.concatenate([piece(r, home) for r in range(count)], axis=1)
        out_ref[home * slots : (home + 1) * slots, :] = lax.dot_general(
            full, weight_ref[...], (((1,), (1,)), ((), ())), preferred_element_type=jnp.float32
        ).astype(jnp.bfloat16)


def mix_kernel(mix_ref, back_ref, out_ref):
    mix = mix_ref[...]
    out_ref[...] = jnp.concatenate(
        [
            jnp.dot(mix, back_ref[c], preferred_element_type=jnp.float32)
            for c in range(back_ref.shape[0])
        ],
        axis=1,
    ).astype(jnp.bfloat16)


def attend(queries, latent_key_cache, fresh_latent_keys, lengths, row_live):
    cache_len = latent_key_cache.shape[1]
    s_old = (
        jnp.einsum("rthc,rkc->rthk", queries, latent_key_cache, preferred_element_type=jnp.float32)
        * score_scale
    )
    s_new = (
        jnp.einsum("rthc,rnc->rthn", queries, fresh_latent_keys, preferred_element_type=jnp.float32)
        * score_scale
    )
    valid_old = jnp.arange(cache_len, dtype=jnp.int32)[None, :] < lengths[:, None]
    valid_new = jnp.arange(2, dtype=jnp.int32)[None, :] <= jnp.arange(2, dtype=jnp.int32)[:, None]
    s_old = jnp.where(valid_old[:, None, None, :], s_old, -jnp.inf)
    s_new = jnp.where(valid_new[None, :, None, :], s_new, -jnp.inf)
    top = jnp.maximum(jnp.max(s_old, -1, keepdims=True), jnp.max(s_new, -1, keepdims=True))
    e_old = jnp.exp(s_old - top)
    e_new = jnp.exp(s_new - top)
    total = jnp.sum(e_old, -1, keepdims=True) + jnp.sum(e_new, -1, keepdims=True)
    cached_probability = (e_old / total).astype(jnp.bfloat16)
    fresh_probability = (e_new / total).astype(jnp.bfloat16)
    out = jnp.einsum(
        "zlim,zmd->zlid",
        cached_probability,
        latent_key_cache[:, :, :LATENT_WIDTH],
        preferred_element_type=jnp.float32,
    )
    out = out + jnp.einsum(
        "swbd,sdo->swbo",
        fresh_probability,
        fresh_latent_keys[:, :, :LATENT_WIDTH],
        preferred_element_type=jnp.float32,
    )
    return (out * row_live.astype(jnp.float32)[:, :, None, None]).astype(jnp.bfloat16)


def per_device(
    queries,
    latent_key_cache,
    fresh_latent_keys,
    lengths,
    accepted,
    hidden,
    norm_gain,
    expert_ids,
    router_weights,
    gate_weight,
    up_weight,
    down_weight,
):
    nreq = queries.shape[0]
    width = hidden.shape[2]
    picks = expert_ids.shape[2]
    nrep = lax.axis_size("rep")
    experts = lax.axis_size("ep")
    rows = nreq * 2
    units = gate_weight.shape[2]
    part = width // nrep
    slots = 2 * experts
    row_live = jnp.stack([jnp.ones_like(accepted), accepted], 1)

    tagged, mix = pl.pallas_call(
        prepare_kernel,
        out_shape=(
            jax.ShapeDtypeStruct((rows, width + slots), jnp.bfloat16),
            jax.ShapeDtypeStruct((rows, slots), jnp.bfloat16),
        ),
        in_specs=[VMEM] * 5,
        out_specs=(VMEM, VMEM),
        compiler_params=limit,
        name="prepare",
    )(
        hidden.reshape(rows, width),
        norm_gain.reshape(1, width),
        expert_ids.reshape(rows, picks),
        router_weights.reshape(rows, picks),
        row_live.reshape(rows, 1),
    )

    def dispatch(rows_in):
        return pl.pallas_call(
            dispatch_kernel,
            out_shape=jax.ShapeDtypeStruct((slots, width), jnp.bfloat16),
            in_specs=[VMEM],
            out_specs=VMEM,
            compiler_params=limit,
            name="dispatch",
        )(rows_in).reshape(experts, 2, width)

    def to_experts(buffer):
        return lax.all_to_all(buffer, "ep", split_axis=0, concat_axis=0, tiled=True).reshape(
            slots, width
        )

    def shift(x, by):
        return lax.ppermute(x, "rep", [(i, (i + by) % nrep) for i in range(nrep)])

    both_weight = jnp.concatenate([gate_weight[0], up_weight[0]], axis=1)

    def inner_blocks(before, *blocks):
        n = len(blocks)
        count = n + sum(piece.shape[0] for piece in before)
        return pl.pallas_call(
            partial(inner_kernel, len(before)),
            out_shape=jax.ShapeDtypeStruct((count, slots, units), jnp.bfloat16),
            in_specs=[VMEM] * (1 + len(before) + n),
            out_specs=VMEM,
            compiler_params=limit,
            cost_estimate=pl.CostEstimate(
                flops=4 * n * slots * width * units,
                bytes_accessed=2 * width * (2 * units + n * slots),
                transcendentals=n * slots * units,
            ),
            name="inner",
        )(both_weight, *before, *blocks)

    half = nrep // 2
    far_rows = shift(tagged, half)
    own = to_experts(dispatch(tagged))
    own, far_buffer = lax.optimization_barrier((own, dispatch(far_rows)))
    far = to_experts(far_buffer)
    up_one, down_one = shift(own, 1), shift(own, -1)
    near = inner_blocks([], own, up_one, down_one)
    up_two, down_two = shift(up_one, 1), shift(down_one, -1)
    up_far, down_far = shift(far, 1), shift(far, -1)
    first_places = [0, nrep - 1, 1, half, nrep - 2, 2]
    first = inner_blocks([near], far, up_two, down_two)
    first = lax.all_gather(first, "rep", axis=0, tiled=False)
    last_places = [half - 1, half + 1]
    last = pl.pallas_call(
        last_inner_kernel,
        out_shape=jax.ShapeDtypeStruct((nrep, 2, slots, units), jnp.bfloat16),
        in_specs=[VMEM] * 3,
        out_specs=VMEM,
        compiler_params=limit,
        name="last_inner",
    )(both_weight, up_far, down_far)
    last = lax.all_to_all(last, "rep", split_axis=0, concat_axis=0, tiled=True)
    expert_out = pl.pallas_call(
        partial(down_kernel, first_places, last_places),
        out_shape=jax.ShapeDtypeStruct((nrep * slots, part), jnp.bfloat16),
        in_specs=[VMEM] * 3,
        out_specs=VMEM,
        compiler_params=limit,
        name="down",
    )(first, last, jnp.swapaxes(down_weight[0], 0, 1))
    queries, expert_out = lax.optimization_barrier((queries, expert_out))
    attended = attend(queries, latent_key_cache, fresh_latent_keys, lengths, row_live)
    back = lax.all_to_all(
        expert_out.reshape(nrep * experts, 2, part),
        ("rep", "ep"),
        split_axis=0,
        concat_axis=0,
        tiled=True,
    ).reshape(nrep, slots, part)
    routed = pl.pallas_call(
        mix_kernel,
        out_shape=jax.ShapeDtypeStruct((rows, width), jnp.bfloat16),
        in_specs=[VMEM] * 2,
        out_specs=VMEM,
        compiler_params=limit,
        name="mix",
    )(mix, back)
    return attended, routed.reshape(nreq, 2, width)


def solution(mesh):
    in_specs = (
        P(("rep", "ep"), None, None, None),
        P(("rep", "ep"), None, None),
        P(("rep", "ep"), None, None),
        P(("rep", "ep")),
        P(("rep", "ep")),
        P(("rep", "ep"), None, None),
        P(),
        P(("rep", "ep"), None, None),
        P(("rep", "ep"), None, None),
        P("ep", None, "rep"),
        P("ep", None, "rep"),
        P("ep", None, "rep"),
    )
    out_specs = (P(("rep", "ep"), None, None, None), P(("rep", "ep"), None, None))
    return jax.shard_map(
        per_device, mesh=mesh, in_specs=in_specs, out_specs=out_specs, check_vma=False
    )
```

```python
from functools import partial

import jax
import jax.numpy as jnp
from jax import lax
from jax.experimental import pallas as pl
from jax.experimental.pallas import tpu as pltpu
from jax.sharding import PartitionSpec as P

LATENT_WIDTH = 512

score_scale = 192.0 ** (-0.5)
SMEM = pl.BlockSpec(memory_space=pltpu.SMEM)
HBM = pl.BlockSpec(memory_space=pltpu.HBM)
VMEM = pl.BlockSpec(memory_space=pltpu.VMEM)
limit = pltpu.CompilerParams(vmem_limit_bytes=48 * 1024 * 1024)


def prepare_kernel(
    hidden_hbm, gain_hbm, ids_ref, accepted_ref, rows_ref, out_ref, hidden_ref, gain_ref, sems
):
    copies = [
        pltpu.make_async_copy(hidden_hbm, hidden_ref, sems.at[0]),
        pltpu.make_async_copy(gain_hbm, gain_ref, sems.at[1]),
    ]
    for copy in copies:
        copy.start()
    requests, per, width = hidden_ref.shape
    slots = out_ref.shape[0]
    rows = requests * per
    lane = lax.broadcasted_iota(jnp.int32, (rows, slots), 1)
    row = lax.broadcasted_iota(jnp.int32, (rows, slots), 0)
    named = jnp.zeros((rows, slots), jnp.float32)
    for q in range(requests):
        accepted = jnp.where(accepted_ref[q] != 0, 1.0, 0.0)
        for t in range(per):
            hit = jnp.zeros((rows, slots), jnp.bool_)
            for p in range(ids_ref.shape[2]):
                hit = hit | (lane // 2 == ids_ref[q, t, p])
            named += jnp.where(hit & (row == per * q + t), 1.0 if t == 0 else accepted, 0.0)
    rank = jnp.zeros((rows, slots), jnp.float32)
    for r in range(rows - 1):
        rank += jnp.where(row > r, named[r : r + 1, :], 0.0)
    taken = jnp.where(rank == (lane % 2).astype(jnp.float32), named, 0.0)
    rows_ref[:, width:] = taken.astype(jnp.bfloat16)

    for copy in copies:
        copy.wait()
    x = jnp.concatenate([hidden_ref[q].astype(jnp.float32) for q in range(requests)], axis=0)
    meansq = jnp.mean(x * x, -1, keepdims=True)
    normed = x * lax.rsqrt(meansq + 1e-06) * gain_ref[...].reshape(1, width)
    rows_ref[:, :width] = normed.astype(jnp.bfloat16)
    dispatch_kernel(rows_ref, out_ref)


def dispatch_kernel(rows_ref, out_ref):
    slots, width = out_ref.shape
    taken = rows_ref[:, width:]
    step = 256
    for c in range(0, width, step):
        out_ref[:, c : c + step] = lax.dot_general(
            taken,
            rows_ref[:, c : c + step],
            (((0,), (0,)), ((), ())),
            preferred_element_type=jnp.float32,
        ).astype(jnp.bfloat16)


def weights_kernel(ids_ref, weights_ref, rows_ref, mix_ref):
    rows, slots = mix_ref.shape
    lane = lax.broadcasted_iota(jnp.int32, (rows, slots), 1)
    row = lax.broadcasted_iota(jnp.int32, (rows, slots), 0)
    weight = jnp.zeros((rows, slots), jnp.float32)
    for r in range(rows):
        q, t = r // ids_ref.shape[1], r % ids_ref.shape[1]
        for p in range(ids_ref.shape[2]):
            hit = (row == r) & (lane // 2 == ids_ref[q, t, p])
            weight += jnp.where(hit, weights_ref[q, t, p], 0.0)
    taken = rows_ref[:, rows_ref.shape[1] - slots :].astype(jnp.float32)
    mix_ref[...] = (taken * weight).astype(jnp.bfloat16)


def inner_piece(rows, weight):
    units = weight.shape[1] // 2
    both = jnp.dot(rows, weight, preferred_element_type=jnp.float32)
    g, u = both[:, :units], both[:, units:]
    return (g / (1.0 + jnp.exp(-g)) * u).astype(jnp.bfloat16)


def inner_kernel(have, weight_ref, *refs):
    out_ref = refs[-1]
    at = 0
    for ref in refs[:have]:
        for i in range(ref.shape[0]):
            out_ref[at] = ref[i]
            at += 1
    for rows_ref in refs[have:-1]:
        out_ref[at] = inner_piece(rows_ref[...], weight_ref[...])
        at += 1


def late_inner_kernel(weight_ref, *refs):
    out_ref = refs[-1]
    for i, rows_ref in enumerate(refs[:-1]):
        piece = inner_piece(rows_ref[...], weight_ref[...])
        for r in range(out_ref.shape[0]):
            out_ref[r, i] = piece


def down_kernel(places, *refs):
    *inner_refs, weight_ref, out_ref = refs
    count, slots = inner_refs[0].shape[0], inner_refs[0].shape[2]

    def piece(r, home):
        for ref, here in zip(inner_refs, places):
            if (home - r) % count in here:
                return ref[r, here.index((home - r) % count)]

    for home in range(count):
        full = jnp.concatenate([piece(r, home) for r in range(count)], axis=1)
        out_ref[home * slots : (home + 1) * slots, :] = lax.dot_general(
            full, weight_ref[...], (((1,), (1,)), ((), ())), preferred_element_type=jnp.float32
        ).astype(jnp.bfloat16)


def mix_kernel(mix_ref, back_ref, out_ref):
    mix = mix_ref[...]
    routed = jnp.concatenate(
        [
            jnp.dot(mix, back_ref[c], preferred_element_type=jnp.float32)
            for c in range(back_ref.shape[0])
        ],
        axis=1,
    )
    requests, per, _ = out_ref.shape
    for q in range(requests):
        out_ref[q] = routed[per * q : per * (q + 1), :].astype(jnp.bfloat16)


def attend(queries, latent_key_cache, fresh_latent_keys, lengths, row_live):
    cache_len = latent_key_cache.shape[1]
    s_old = (
        jnp.einsum("rthc,rkc->rthk", queries, latent_key_cache, preferred_element_type=jnp.float32)
        * score_scale
    )
    s_new = (
        jnp.einsum("rthc,rnc->rthn", queries, fresh_latent_keys, preferred_element_type=jnp.float32)
        * score_scale
    )
    valid_old = jnp.arange(cache_len, dtype=jnp.int32)[None, :] < lengths[:, None]
    valid_new = jnp.arange(2, dtype=jnp.int32)[None, :] <= jnp.arange(2, dtype=jnp.int32)[:, None]
    s_old = jnp.where(valid_old[:, None, None, :], s_old, -jnp.inf)
    s_new = jnp.where(valid_new[None, :, None, :], s_new, -jnp.inf)
    top = jnp.maximum(jnp.max(s_old, -1, keepdims=True), jnp.max(s_new, -1, keepdims=True))
    e_old = jnp.exp(s_old - top)
    e_new = jnp.exp(s_new - top)
    total = jnp.sum(e_old, -1, keepdims=True) + jnp.sum(e_new, -1, keepdims=True)
    cached_probability = (e_old / total).astype(jnp.bfloat16)
    fresh_probability = (e_new / total).astype(jnp.bfloat16)
    out = jnp.einsum(
        "zlim,zmd->zlid",
        cached_probability,
        latent_key_cache[:, :, :LATENT_WIDTH],
        preferred_element_type=jnp.float32,
    )
    out = out + jnp.einsum(
        "swbd,sdo->swbo",
        fresh_probability,
        fresh_latent_keys[:, :, :LATENT_WIDTH],
        preferred_element_type=jnp.float32,
    )
    return (out * row_live.astype(jnp.float32)[:, :, None, None]).astype(jnp.bfloat16)


def per_device(
    queries,
    latent_key_cache,
    fresh_latent_keys,
    lengths,
    accepted,
    hidden,
    norm_gain,
    expert_ids,
    router_weights,
    gate_weight,
    up_weight,
    down_weight,
):
    nreq = queries.shape[0]
    width = hidden.shape[2]
    nrep = lax.axis_size("rep")
    experts = lax.axis_size("ep")
    rows = nreq * 2
    units = gate_weight.shape[2]
    part = width // nrep
    slots = 2 * experts
    row_live = jnp.stack([jnp.ones_like(accepted), accepted], 1)

    tagged, buffer = pl.pallas_call(
        prepare_kernel,
        out_shape=(
            jax.ShapeDtypeStruct((rows, width + slots), jnp.bfloat16),
            jax.ShapeDtypeStruct((slots, width), jnp.bfloat16),
        ),
        in_specs=[HBM, HBM, SMEM, SMEM],
        out_specs=(VMEM,) * 2,
        scratch_shapes=[
            pltpu.VMEM(hidden.shape, hidden.dtype),
            pltpu.VMEM(norm_gain.shape, norm_gain.dtype),
            pltpu.SemaphoreType.DMA((2,)),
        ],
        compiler_params=limit,
        name="prepare",
    )(hidden, norm_gain, expert_ids, accepted)
    mix = pl.pallas_call(
        weights_kernel,
        out_shape=jax.ShapeDtypeStruct((rows, slots), jnp.bfloat16),
        in_specs=[SMEM, SMEM, VMEM],
        out_specs=VMEM,
        compiler_params=limit,
        name="weights",
    )(expert_ids, router_weights.astype(jnp.float32), tagged)

    def to_experts(buffer):
        columns = buffer.shape[1]
        return lax.all_to_all(
            buffer.reshape(experts, 2, columns), "ep", split_axis=0, concat_axis=0, tiled=True
        ).reshape(slots, columns)

    def shift(x, by):
        return lax.ppermute(x, "rep", [(i, (i + by) % nrep) for i in range(nrep)])

    both_weight = jnp.concatenate([gate_weight[0], up_weight[0]], axis=1)

    def inner_blocks(before, *blocks):
        n = len(blocks)
        count = n + sum(piece.shape[0] for piece in before)
        return pl.pallas_call(
            partial(inner_kernel, len(before)),
            out_shape=jax.ShapeDtypeStruct((count, slots, units), jnp.bfloat16),
            in_specs=[VMEM] * (1 + len(before) + n),
            out_specs=VMEM,
            compiler_params=limit,
            name="inner",
        )(both_weight, *before, *blocks)

    def dispatch(rows_in):
        return pl.pallas_call(
            dispatch_kernel,
            out_shape=jax.ShapeDtypeStruct((slots, width), jnp.bfloat16),
            in_specs=[VMEM],
            out_specs=VMEM,
            compiler_params=limit,
            name="dispatch",
        )(rows_in)

    half = nrep // 2
    far_rows = shift(tagged, half)
    own = to_experts(buffer)
    own, far_buffer = lax.optimization_barrier((own, dispatch(far_rows)))
    up_one, down_one = shift(own, 1), shift(own, -1)
    at_home, far_buffer = lax.optimization_barrier((inner_blocks([], own), far_buffer))
    far = to_experts(far_buffer)
    near = inner_blocks([at_home], up_one, down_one)
    up_two, down_two = shift(up_one, 1), shift(down_one, -1)
    up_far, down_far = shift(far, 1), shift(far, -1)
    first_places = [0, nrep - 1, 1, half]
    first = lax.all_gather(inner_blocks([near], far), "rep", axis=0, tiled=False)

    def late_blocks(*blocks):
        pieces = pl.pallas_call(
            late_inner_kernel,
            out_shape=jax.ShapeDtypeStruct((nrep, len(blocks), slots, units), jnp.bfloat16),
            in_specs=[VMEM] * (1 + len(blocks)),
            out_specs=VMEM,
            compiler_params=limit,
            name="late_inner",
        )(both_weight, *blocks)
        return lax.all_to_all(pieces, "rep", split_axis=0, concat_axis=0, tiled=True)

    second, third = late_blocks(up_two, down_two), late_blocks(up_far, down_far)
    places = [first_places, [nrep - 2, 2], [half - 1, half + 1]]
    expert_out = pl.pallas_call(
        partial(down_kernel, places),
        out_shape=jax.ShapeDtypeStruct((nrep * slots, part), jnp.bfloat16),
        in_specs=[VMEM] * 4,
        out_specs=VMEM,
        compiler_params=limit,
        name="down",
    )(first, second, third, jnp.swapaxes(down_weight[0], 0, 1))
    queries, expert_out = lax.optimization_barrier((queries, expert_out))
    attended = attend(queries, latent_key_cache, fresh_latent_keys, lengths, row_live)
    back = lax.all_to_all(
        expert_out.reshape(nrep * experts, 2, part),
        ("rep", "ep"),
        split_axis=0,
        concat_axis=0,
        tiled=True,
    ).reshape(nrep, slots, part)
    routed = pl.pallas_call(
        mix_kernel,
        out_shape=jax.ShapeDtypeStruct((nreq, 2, width), jnp.bfloat16),
        in_specs=[VMEM] * 2,
        out_specs=VMEM,
        compiler_params=limit,
        name="mix",
    )(mix, back)
    return attended, routed


def solution(mesh):
    in_specs = (
        P(("rep", "ep"), None, None, None),
        P(("rep", "ep"), None, None),
        P(("rep", "ep"), None, None),
        P(("rep", "ep")),
        P(("rep", "ep")),
        P(("rep", "ep"), None, None),
        P(),
        P(("rep", "ep"), None, None),
        P(("rep", "ep"), None, None),
        P("ep", None, "rep"),
        P("ep", None, "rep"),
        P("ep", None, "rep"),
    )
    out_specs = (P(("rep", "ep"), None, None, None), P(("rep", "ep"), None, None))
    return jax.shard_map(
        per_device, mesh=mesh, in_specs=in_specs, out_specs=out_specs, check_vma=False
    )
```
